32 devices in a mesh: groups: 2 (over y), length: 4 (over z), sector: 2 (over x), pair: 2 (over core).
Axes of the slice: x: 2, y: 2, z: 4, core: 2. Of those that a mesh axis runs over, the one named last changes fastest.
Arguments:
- flag_kernels: bfloat16 [4, 8, 32, 25, 1024], P('length', ('groups', 'sector', 'pair')), parts along dimension 1, may hold values from -1.1953125 to 1.1953125
- flag_unary: bfloat16 [4, 8, 32, 8, 1024], P('length', ('groups', 'sector', 'pair')), parts along dimension 1, may hold values from -8 to 8
- flag_labels: int32 [4, 8, 32, 1024], P('length', ('groups', 'sector', 'pair')), parts along dimension 1, may hold values from 0 to 7
- flag_mask: int32 [4, 8, 32, 1024], P('length', ('groups', 'sector', 'pair')), parts along dimension 1, may hold values 0 or 1
- dest_list: int32 [4, 8, 32], P('length', ('groups', 'sector', 'pair')), parts along dimension 1, may hold values from -1 to 3, as said below
- slot_list: int32 [4, 8, 32], P('length', ('groups', 'sector', 'pair')), parts along dimension 1, may hold values from -1 to 15, as said below
- res_kernels: bfloat16 [4, 8, 8, 25, 1024], P('length', ('groups', 'sector', 'pair')), parts along dimension 1, may hold values from -1.1953125 to 1.1953125
- res_unary: bfloat16 [4, 8, 8, 8, 1024], P('length', ('groups', 'sector', 'pair')), parts along dimension 1, may hold values from -8 to 8
- res_labels: int32 [4, 8, 8, 1024], P('length', ('groups', 'sector', 'pair')), parts along dimension 1, may hold values from 0 to 7
- res_mask: int32 [4, 8, 8, 1024], P('length', ('groups', 'sector', 'pair')), parts along dimension 1, may hold values 0 or 1
Outputs:
- flag_grad: bfloat16 [4, 8, 32, 25, 1024], P('length', ('groups', 'sector', 'pair')), parts along dimension 1
- res_grad: bfloat16 [4, 8, 8, 25, 1024], P('length', ('groups', 'sector', 'pair')), parts along dimension 1
- helper_loss: float32 [4, 8, 16], P('length', ('groups', 'sector', 'pair')), parts along dimension 1
The draws below stay inside these ranges and needn't reach their ends.
There are 2 independent parts, one for each index of `groups`. The reference program is written for one: setup_inputs(seed, part) draws one part's arguments, and reference() takes and returns one part's arrays. A program takes and returns all parts, laid end to end along the dimension named above; each array names one. Nothing has to cross between parts.
Inputs may be any that keep to these rules, and one draw needn't show every extreme that they name: `dest_list`: entry j of a device's list is -1 exactly when its slot j holds no flagged tile, and the -1 entries come after all others; at most 8 entries of one device name the same destination. `slot_list`: for each index along sector and pair, each pair of a destination along length and a slot 0 to 15 is named by exactly one entry of the lists of the devices along length; an entry is -1 exactly where dest_list is -1.
All inputs are finite; a program needn't handle non-finite values. No bound on the sum of `flag_mask` or of `res_mask` on one device may be relied on, other than what follows from the above.
Results may differ from the reference program's by a relative error of at most 0.001.
Values may be sent and summed in bfloat16 or wider, within the bound.
A program may use at most 64 MiB of HBM per device.

```python
import jax
import jax.numpy as jnp
from jax import lax

CLASSES = 8
TAPS = 25
TILE = 32
ITERS = 3
FLAG_MAX = 32
RES = 8
PIX = 1024
NSP = 4
RECV = 16
N_LENGTH = 4
N_SECTOR = 2
N_PAIR = 2


def shuffle_slots(subkey):
    return jax.random.permutation(subkey, RECV)


def list_tables(key):
    device_count = N_LENGTH
    groups = N_SECTOR * N_PAIR

    def one_group(group_key):
        subkeys = jax.random.split(group_key, 6)
        spread = jax.random.randint(subkeys[0], (device_count // 2,), 0, RECV + 1)
        chosen = jax.random.randint(subkeys[1], (), 0, device_count // 2)
        spread = jnp.where(jnp.arange(device_count // 2) == chosen, RECV, spread)
        flip_sign = 2 * jax.random.randint(subkeys[2], (device_count // 2,), 0, 2) - 1
        paired = jnp.stack([RECV + flip_sign * spread, RECV - flip_sign * spread], axis=1).reshape(device_count)
        tile_loads = paired[jax.random.permutation(subkeys[3], device_count)]
        starts = jnp.cumsum(tile_loads) - tile_loads
        slot_order = jnp.arange(FLAG_MAX)
        global_index = starts[:, None] + slot_order[None, :]
        listed = slot_order[None, :] < tile_loads[:, None]
        rotation = jax.random.randint(subkeys[4], (), 0, device_count)
        target = (global_index + rotation) % device_count
        shuffles = jax.vmap(shuffle_slots)(jax.random.split(subkeys[5], device_count))
        slot_place = shuffles[target, jnp.minimum(global_index // device_count, RECV - 1)]
        return (jnp.where(listed, target, -1).astype(jnp.int32), jnp.where(listed, slot_place, -1).astype(jnp.int32))
    destinations, slot_names = jax.vmap(one_group)(jax.random.split(key, groups))
    return (jnp.transpose(destinations, (1, 0, 2)), jnp.transpose(slot_names, (1, 0, 2)))


def draw_dest_list(key, part):
    return list_tables(jax.random.fold_in(key, 11))[0]


def draw_slot_list(key, part):
    return list_tables(jax.random.fold_in(key, 11))[1]


def set_ends(array, own_key, low, high):
    shape = array.shape
    place = [jax.random.randint(jax.random.fold_in(own_key, axis), (), 0, shape[axis]) for axis in range(len(shape))]
    array = array.at[tuple(place)].set(low)
    longest = shape.index(max(shape))
    place[longest] = (place[longest] + 1) % shape[longest]
    return array.at[tuple(place)].set(high)


def block_levels(key, extent, cuts, least, top_value):
    gain, own = 1.0, jax.random.fold_in(key, 6)
    for dim, shards_of in cuts:
        draws = jnp.exp(jax.random.uniform(jax.random.fold_in(own, dim), (shards_of,), jnp.float32, least / len(cuts), top_value / len(cuts)))
        gain = gain * jnp.repeat(draws, extent[dim] // shards_of).reshape([-1 if axis == dim else 1 for axis in range(len(extent))])
    return gain


def gaussian(own_key, dims, width, bound, cuts=(), dtype=jnp.bfloat16):
    result = width * jax.random.normal(own_key, dims, jnp.float32)
    if cuts:
        result = result * block_levels(own_key, dims, cuts, -0.22, 0.18)
    return jnp.clip(result, -bound, bound).astype(dtype)


def setup_inputs(seed: int = 0, part: int = 0) -> dict:
    arg_keys = jax.random.split(jax.random.key(seed), 11)
    part_keys = jax.random.split(jax.random.fold_in(arg_keys[10], part), 11)
    flag_kernels = gaussian(part_keys[0], (N_LENGTH, NSP, FLAG_MAX, TAPS, PIX), 0.2, 1.1953125, ((0, 4), (1, 4)))
    flag_unary = gaussian(part_keys[1], (N_LENGTH, NSP, FLAG_MAX, CLASSES, PIX), 2.0, 8.0, ((0, 4), (1, 4)))
    flag_labels = set_ends(jax.random.randint(part_keys[2], (N_LENGTH, NSP, FLAG_MAX, PIX), 0, CLASSES), jax.random.fold_in(part_keys[2], 1), 0, CLASSES - 1).astype(jnp.int32)
    flag_mask = set_ends((jax.random.randint(part_keys[3], (N_LENGTH, NSP, FLAG_MAX, PIX), 0, 4) < 3).astype(jnp.int32), jax.random.fold_in(part_keys[3], 1), 0, 1)
    dest_list = draw_dest_list(jax.random.fold_in(jax.random.fold_in(arg_keys[10], part), 71), part)
    slot_list = draw_slot_list(jax.random.fold_in(jax.random.fold_in(arg_keys[10], part), 71), part)
    res_kernels = gaussian(part_keys[6], (N_LENGTH, NSP, RES, TAPS, PIX), 0.2, 1.1953125, ((0, 4), (1, 4)))
    res_unary = gaussian(part_keys[7], (N_LENGTH, NSP, RES, CLASSES, PIX), 2.0, 8.0, ((0, 4), (1, 4)))
    res_labels = set_ends(jax.random.randint(part_keys[8], (N_LENGTH, NSP, RES, PIX), 0, CLASSES), jax.random.fold_in(part_keys[8], 1), 0, CLASSES - 1).astype(jnp.int32)
    res_mask = set_ends((jax.random.randint(part_keys[9], (N_LENGTH, NSP, RES, PIX), 0, 4) < 3).astype(jnp.int32), jax.random.fold_in(part_keys[9], 1), 0, 1)
    return {"flag_kernels": flag_kernels, "flag_unary": flag_unary, "flag_labels": flag_labels, "flag_mask": flag_mask, "dest_list": dest_list, "slot_list": slot_list, "res_kernels": res_kernels, "res_unary": res_unary, "res_labels": res_labels, "res_mask": res_mask}


def normalize(logits):
    raised = jnp.exp(logits)
    return raised / lax.optimization_barrier(jnp.sum(raised, axis=0, keepdims=True))

def message(field_values, tap_weights):
    tile_side = TILE
    pixels = tile_side * tile_side
    margin = 2 * tile_side + 2
    padded = jnp.pad(field_values, ((0, 0), (margin, margin)))
    column = jnp.arange(pixels) % tile_side
    summed = jnp.zeros_like(field_values)
    tap_index = 0
    for row_step in range(-2, 3):
        for col_step in range(-2, 3):
            offset = row_step * tile_side + col_step
            shifted = lax.slice_in_dim(padded, margin + offset, margin + offset + pixels, axis=1)
            inside = ((column + col_step >= 0) & (column + col_step < tile_side)).astype(jnp.float32)
            summed = summed + (tap_weights[tap_index] * inside)[None, :] * shifted
            tap_index += 1
    return summed

def tile_objective(tap_weights, unary_terms, labels, weights):
    unary_terms = unary_terms.astype(jnp.float32)
    beliefs = normalize(unary_terms)
    logits = unary_terms
    for sweep_index in range(ITERS):
        logits = unary_terms + message(beliefs, tap_weights)
        if sweep_index + 1 < ITERS:
            beliefs = normalize(logits)
    summed = jnp.log(lax.optimization_barrier(jnp.sum(jnp.exp(logits), axis=0)))
    chosen = lax.optimization_barrier(jnp.sum(jnp.where(jnp.arange(CLASSES)[:, None] == labels[None, :], logits, 0.0), axis=0))
    return jnp.sum(weights * (summed - chosen))

def tile_work(tap_weights, unary_terms, labels, weights):
    total_value, gradient = jax.value_and_grad(tile_objective)(tap_weights.astype(jnp.float32), unary_terms, labels, weights)
    return (total_value / TILE, gradient.astype(jnp.bfloat16))

def batched(tap_weights, unary_terms, labels, weights, block_size):
    amount = tap_weights.shape[0]

    def compute_block(group_arrays):
        return jax.vmap(tile_work)(*group_arrays)
    shaped = tuple((member.reshape((amount // block_size, block_size) + member.shape[1:]) for member in (tap_weights, unary_terms, labels, weights)))
    losses, slopes = lax.map(compute_block, shaped)
    return (losses.reshape(amount), slopes.reshape((amount,) + slopes.shape[2:]))

def run_tiles(kernels, unary, labels, mask):
    leading = kernels.shape[:3]
    losses, slopes = batched(kernels.reshape((-1,) + kernels.shape[3:]), unary.reshape((-1,) + unary.shape[3:]), labels.reshape((-1, labels.shape[3])), mask.reshape((-1, mask.shape[3])).astype(jnp.float32), 16)
    return (losses.reshape(leading), slopes.reshape(kernels.shape))

def reference(flag_kernels, flag_unary, flag_labels, flag_mask, dest_list, slot_list, res_kernels, res_unary, res_labels, res_mask):
    flag_losses, flag_slopes = run_tiles(flag_kernels, flag_unary, flag_labels, flag_mask)
    resident_losses, resident_slopes = run_tiles(res_kernels, res_unary, res_labels, res_mask)
    is_listed = dest_list >= 0
    flag_grad = jnp.where(is_listed[..., None, None], flag_slopes, jnp.zeros_like(flag_slopes))
    leading = dest_list.shape
    row_index = jnp.where(is_listed, dest_list, N_LENGTH).astype(jnp.int32)
    columns = jnp.broadcast_to(jnp.arange(leading[1]).astype(jnp.int32)[None, :, None], leading)
    slot_index = jnp.where(is_listed, slot_list, 0).astype(jnp.int32)
    helper_loss = jnp.zeros((N_LENGTH, leading[1], RECV), jnp.float32).at[row_index, columns, slot_index].set(flag_losses, mode='drop')
    return (flag_grad, resident_slopes, helper_loss)
```

```python
import functools

import jax
import jax.numpy as jnp
from jax import lax
from jax.experimental import pallas as pl
from jax.experimental.pallas import tpu as pltpu
from jax.sharding import PartitionSpec as P

CLASSES = 8
TAPS = 25
TILE = 32
ITERS = 3
RECV = 16
STEP = 8

OFFSETS = [(a, b) for a in range(-2, 3) for b in range(-2, 3)]


def shift_all(x, lane):
    after = pltpu.roll(x, 7, 0)
    before = pltpu.roll(x, 1, 0)
    shifted = []
    for a, b in OFFSETS:
        k = a * TILE + b
        if k == 0:
            shifted.append(x)
        elif k > 0:
            shifted.append(pltpu.roll(jnp.where(lane >= k, x, after), 128 - k, 1))
        else:
            shifted.append(pltpu.roll(jnp.where(lane < 128 + k, x, before), -k, 1))
    return shifted


def shift_one(x, k, lane):
    if k == 0:
        return x
    if k > 0:
        return pltpu.roll(jnp.where(lane >= k, x, pltpu.roll(x, 7, 0)), 128 - k, 1)
    return pltpu.roll(jnp.where(lane < 128 + k, x, pltpu.roll(x, 1, 0)), -k, 1)


def total(values):
    while len(values) > 1:
        values = [sum(values[i : i + 2]) for i in range(0, len(values), 2)]
    return values[0]


def tile(j, k_ref, u_ref, tgt_ref, grad_ref, loss_ref, flat, unary, kfwd, kbwd, shf):
    lane = lax.broadcasted_iota(jnp.int32, (8, 128), 1)
    sub = lax.broadcasted_iota(jnp.int32, (8, 128), 0)
    row = sub * 4 + lane // TILE
    col = lane % TILE

    def inside(t):
        a, b = OFFSETS[t]
        return (row + a >= 0) & (row + a < TILE) & (col + b >= 0) & (col + b < TILE)

    for p in range(8):
        part = slice(128 * p, 128 * (p + 1))
        flat[pl.ds(p, TAPS, stride=8), :] = k_ref[0, 0, j, :, part].astype(jnp.float32)
        unary[pl.ds(p, CLASSES, stride=8), :] = u_ref[0, 0, j, :, part].astype(jnp.float32)
    for t in range(TAPS):
        a, b = OFFSETS[t]
        masked = jnp.where(inside(t), flat[8 * t : 8 * t + 8, :], 0.0)
        kfwd[t] = masked
        kbwd[TAPS - 1 - t] = shift_one(masked, -(a * TILE + b), lane)

    def send(field, weights, keep):
        result = []
        for c in range(CLASSES):
            moved = shift_all(field[c], lane)
            if keep is not None:
                for t in range(TAPS):
                    shf[keep, t, c] = moved[t]
            sums = [moved[t] * weights[t] for t in range(5)]
            for t in range(5, TAPS):
                sums[t % 5] = sums[t % 5] + moved[t] * weights[t]
            result.append(total(sums))
        return result

    def soft(logits):
        raised = [jnp.exp(x) for x in logits]
        summed = total(raised)
        scale = 1.0 / summed
        return [x * scale for x in raised], summed

    first = [unary[8 * c : 8 * c + 8, :] for c in range(CLASSES)]
    beliefs, _ = soft(first)
    kept = [beliefs]
    for i in range(ITERS):
        sent = send(beliefs, kfwd, i)
        logits = [unary[8 * c : 8 * c + 8, :] + sent[c] for c in range(CLASSES)]
        beliefs, summed = soft(logits)
        kept.append(beliefs)
    labels = tgt_ref[j]
    used = labels < CLASSES
    chosen = total([jnp.where(labels == c, logits[c], 0.0) for c in range(CLASSES)])
    loss_ref[j] = jnp.where(used, jnp.log(summed) - chosen, 0.0)
    slope = [
        jnp.where(used, kept[3][c] - jnp.where(labels == c, 1.0, 0.0), 0.0)
        for c in range(CLASSES)
    ]
    slopes = [None, None, slope]
    for i in (1, 0):
        back = send(slopes[i + 1], kbwd, None)
        field = kept[i + 1]
        mean = total([field[c] * back[c] for c in range(CLASSES)])
        slopes[i] = [field[c] * (back[c] - mean) for c in range(CLASSES)]
    for t in range(TAPS):
        gathered = total(
            [slopes[i][c] * shf[i, t, c] for i in range(ITERS) for c in range(CLASSES)]
        )
        flat[8 * t : 8 * t + 8, :] = jnp.where(inside(t), gathered, 0.0)
    for p in range(8):
        grad_ref[0, 0, j, :, 128 * p : 128 * (p + 1)] = flat[
            pl.ds(p, TAPS, stride=8), :
        ].astype(jnp.bfloat16)


def crf_kernel(dest_ref, k_ref, u_ref, tgt_ref, grad_ref, loss_ref, *scratch):
    base = pl.program_id(0) * STEP

    @pl.loop(0, STEP)
    def _(j):
        listed = dest_ref[base + j] >= 0

        @pl.when(listed)
        def _():
            tile(j, k_ref, u_ref, tgt_ref, grad_ref, loss_ref, *scratch)

        @pl.when(jnp.logical_not(listed))
        def _():
            grad_ref[0, 0, j] = jnp.zeros(grad_ref.shape[3:], grad_ref.dtype)
            loss_ref[j] = jnp.zeros((8, 128), jnp.float32)


def crf(listed, kernels, unary, labels, mask):
    amount, taps, pixels = kernels.shape[2:]
    big = lambda d: pl.BlockSpec((1, 1, STEP, d, pixels), lambda i, s: (0, 0, i, 0, 0))
    flat = pl.BlockSpec((STEP, 8, 128), lambda i, s: (i, 0, 0))
    target = jnp.where(mask == 1, labels, CLASSES).reshape(amount, 8, 128)
    return pl.pallas_call(
        crf_kernel,
        grid_spec=pltpu.PrefetchScalarGridSpec(
            num_scalar_prefetch=1,
            grid=(amount // STEP,),
            in_specs=[big(taps), big(CLASSES), flat],
            out_specs=[big(taps), flat],
            scratch_shapes=[
                pltpu.VMEM((TAPS * 8, 128), jnp.float32),
                pltpu.VMEM((CLASSES * 8, 128), jnp.float32),
                pltpu.VMEM((TAPS, 8, 128), jnp.float32),
                pltpu.VMEM((TAPS, 8, 128), jnp.float32),
                pltpu.VMEM((ITERS, TAPS, CLASSES, 8, 128), jnp.float32),
            ],
        ),
        out_shape=[
            jax.ShapeDtypeStruct(kernels.shape, jnp.bfloat16),
            jax.ShapeDtypeStruct((amount, 8, 128), jnp.float32),
        ],
        compiler_params=pltpu.CompilerParams(vmem_limit_bytes=24 * 1024 * 1024),
    )(listed, kernels, unary, target)


def on_device(fk, fu, fl, fm, dest, slot, rk, ru, rl, rm):
    destinations, slots = dest[0, 0], slot[0, 0]
    flag_grad, partial = crf(destinations, fk, fu, fl, fm)
    count = lax.axis_size("length")
    losses = jnp.sum(partial, axis=(1, 2)) / TILE
    place = jnp.where(destinations >= 0, destinations * RECV + slots, -1)
    table = jnp.sum(
        jnp.where(place[None, :] == jnp.arange(count * RECV)[:, None], losses[None, :], 0.0), axis=1
    )
    got = lax.all_to_all(
        table.reshape(count, RECV), "length", split_axis=0, concat_axis=0, tiled=True
    )
    res_grad, _ = crf(jnp.zeros((rk.shape[2],), jnp.int32), rk, ru, rl, rm)
    return flag_grad, res_grad, jnp.sum(got, axis=0)[None, None]


def solution(mesh):
    tile_axes = ("groups", "sector", "pair")
    spec = lambda n: P("length", tile_axes, *([None] * n))
    return jax.shard_map(
        on_device,
        mesh=mesh,
        in_specs=(spec(3), spec(3), spec(2), spec(2), spec(1), spec(1), spec(3), spec(3), spec(2), spec(2)),
        out_specs=(spec(3), spec(3), spec(1)),
        check_vma=False,
    )
```

```python
import functools

import jax
import jax.numpy as jnp
from jax import lax
from jax.experimental import pallas as pl
from jax.experimental.pallas import tpu as pltpu
from jax.sharding import PartitionSpec as P

CLASSES = 8
TAPS = 25
TILE = 32
ITERS = 3
RECV = 16
STEP = 8
PAD = 8
ROWS = TILE + 2 * PAD

OFFSETS = [(a, b) for a in range(-2, 3) for b in range(-2, 3)]


def total(values):
    while len(values) > 1:
        values = [sum(values[i : i + 2]) for i in range(0, len(values), 2)]
    return values[0]


def by_block(block, values):
    return jnp.where(
        block < 2,
        jnp.where(block == 0, values[0], values[1]),
        jnp.where(block == 2, values[2], values[3]),
    )


def turn(x, amount):
    amount %= 128
    return pltpu.roll(x, amount, 1) if amount else x


def tile(j, k_ref, u_ref, tgt_ref, grad_ref, loss_ref, flat, unary, krep, fields, slopes, work):
    lane = lax.broadcasted_iota(jnp.int32, (8, 128), 1)
    block = lane // TILE
    col = lane % TILE
    valid = {b: (col + b >= 0) & (col + b < TILE) for b in (-2, -1, 1, 2)}
    parts = range(4)
    groups = range(2)

    def mask(x, b):
        return jnp.where(valid[b], x, 0.0) if b else x

    for p in range(8):
        part = slice(128 * p, 128 * (p + 1))
        flat[pl.ds(p, TAPS, stride=8), :] = k_ref[0, 0, j, :, part].astype(jnp.float32)
        unary[pl.ds(p, CLASSES, stride=8), :] = u_ref[0, 0, j, :, part].astype(jnp.float32)
    for t in range(TAPS):
        x = mask(flat[8 * t : 8 * t + 8, :], OFFSETS[t][1])
        turned = [turn(x, TILE * d) for d in range(4)]
        for q in range(4):
            krep[pl.ds(t * ROWS + PAD + q, 8, stride=4), :] = by_block(
                block, [turned[(p - q) % 4] for p in range(4)]
            )
    for g in groups:
        for q in range(4):
            work[pl.ds(g * TILE + q, 8, stride=4), :] = by_block(
                block,
                [
                    turn(unary[8 * (4 * g + p) : 8 * (4 * g + p) + 8, :], TILE * (p - q))
                    for p in range(4)
                ],
            )
    wanted = tgt_ref[j]
    turned = [turn(wanted, TILE * d) for d in range(4)]
    for q in range(4):
        work[pl.ds(2 * TILE + q, 8, stride=4), :] = by_block(
            block, [turned[(p - q) % 4] for p in range(4)]
        )
    scores = [[work[g * TILE + 8 * v : g * TILE + 8 * v + 8, :] for v in parts] for g in groups]

    def over_classes(x):
        x = x + turn(x, 64)
        return x + turn(x, 32)

    def soft(logits):
        raised = [[jnp.exp(x) for x in logits[g]] for g in groups]
        summed = [over_classes(raised[0][v] + raised[1][v]) for v in parts]
        scale = [1.0 / x for x in summed]
        return [[raised[g][v] * scale[v] for v in parts] for g in groups], summed

    kept = []
    beliefs, _ = soft(scores)
    for i in range(ITERS):
        kept.append(beliefs)
        for g in groups:
            for v in parts:
                for b in range(-2, 3):
                    fields[i, g, b + 2, PAD + 8 * v : PAD + 8 * v + 8, :] = turn(
                        beliefs[g][v], -b
                    )
        logits = [[None] * 4 for _ in groups]
        for v in parts:
            sums = [[None] * 5 for _ in groups]
            for t, (a, b) in enumerate(OFFSETS):
                base = t * ROWS + PAD + 8 * v
                weight = krep[base : base + 8, :]
                for g in groups:
                    start = PAD + 8 * v + a
                    term = weight * fields[i, g, b + 2, start : start + 8, :]
                    sums[g][a + 2] = term if b == -2 else sums[g][a + 2] + term
            for g in groups:
                logits[g][v] = scores[g][v] + total(sums[g])
        beliefs, summed = soft(logits)
    kept.append(beliefs)
    loss = jnp.zeros((8, 128), jnp.float32)
    slope = [[None] * 4 for _ in groups]
    for v in parts:
        label = work[2 * TILE + 8 * v : 2 * TILE + 8 * v + 8, :]
        used = label < float(CLASSES)
        value = jnp.where(block == 0, jnp.log(summed[v]), 0.0)
        for g in groups:
            hit = label == (block + 4 * g).astype(jnp.float32)
            value = value - jnp.where(hit, logits[g][v], 0.0)
            slope[g][v] = jnp.where(used, beliefs[g][v] - jnp.where(hit, 1.0, 0.0), 0.0)
        loss = loss + jnp.where(used, value, 0.0)
    loss_ref[j] = loss
    for i in (2, 1, 0):
        for g in groups:
            for v in parts:
                slopes[i, g, PAD + 8 * v : PAD + 8 * v + 8, :] = slope[g][v]
        if i == 0:
            break
        back = [[None] * 4 for _ in groups]
        for v in parts:
            moved = [[None] * 5 for _ in groups]
            for a in range(-2, 3):
                start = PAD + 8 * v - a
                here = [slopes[i, g, start : start + 8, :] for g in groups]
                for b in range(-2, 3):
                    base = (5 * (a + 2) + b + 2) * ROWS + start
                    weight = krep[base : base + 8, :]
                    for g in groups:
                        term = weight * here[g]
                        moved[g][b + 2] = term if a == -2 else moved[g][b + 2] + term
            for g in groups:
                back[g][v] = total([turn(moved[g][b + 2], b) for b in range(-2, 3)])
        slope = [[None] * 4 for _ in groups]
        for v in parts:
            mean = over_classes(total([kept[i][g][v] * back[g][v] for g in groups]))
            for g in groups:
                slope[g][v] = kept[i][g][v] * (back[g][v] - mean)
    for v in parts:
        here = [[slopes[i, g, PAD + 8 * v : PAD + 8 * v + 8, :] for g in groups] for i in range(ITERS)]
        for t, (a, b) in enumerate(OFFSETS):
            start = PAD + 8 * v + a
            gathered = total(
                [
                    here[i][g] * fields[i, g, b + 2, start : start + 8, :]
                    for i in range(ITERS)
                    for g in groups
                ]
            )
            base = t * ROWS + PAD + 8 * v
            krep[base : base + 8, :] = gathered
    for t in range(TAPS):
        rows = [krep[pl.ds(t * ROWS + PAD + q, 8, stride=4), :] for q in range(4)]
        found = total(
            [turn(by_block(block, [rows[(p + d) % 4] for p in range(4)]), TILE * d) for d in range(4)]
        )
        flat[8 * t : 8 * t + 8, :] = mask(found, OFFSETS[t][1])
    for p in range(8):
        grad_ref[0, 0, j, :, 128 * p : 128 * (p + 1)] = flat[
            pl.ds(p, TAPS, stride=8), :
        ].astype(jnp.bfloat16)


def crf_kernel(dest_ref, k_ref, u_ref, tgt_ref, grad_ref, loss_ref, *scratch):
    base = pl.program_id(0) * STEP

    @pl.when(base == 0)
    def _():
        for ref in scratch[2:5]:
            ref[...] = jnp.zeros(ref.shape, ref.dtype)

    @pl.loop(0, STEP)
    def _(j):
        listed = dest_ref[base + j] >= 0

        @pl.when(listed)
        def _():
            tile(j, k_ref, u_ref, tgt_ref, grad_ref, loss_ref, *scratch)

        @pl.when(jnp.logical_not(listed))
        def _():
            grad_ref[0, 0, j] = jnp.zeros(grad_ref.shape[3:], grad_ref.dtype)
            loss_ref[j] = jnp.zeros((8, 128), jnp.float32)


def crf(listed, kernels, unary, labels, mask):
    amount, taps, pixels = kernels.shape[2:]
    big = lambda d: pl.BlockSpec((1, 1, STEP, d, pixels), lambda i, s: (0, 0, i, 0, 0))
    flat = pl.BlockSpec((STEP, 8, 128), lambda i, s: (i, 0, 0))
    target = jnp.where(mask == 1, labels, CLASSES).astype(jnp.float32).reshape(amount, 8, 128)
    return pl.pallas_call(
        crf_kernel,
        grid_spec=pltpu.PrefetchScalarGridSpec(
            num_scalar_prefetch=1,
            grid=(amount // STEP,),
            in_specs=[big(taps), big(CLASSES), flat],
            out_specs=[big(taps), flat],
            scratch_shapes=[
                pltpu.VMEM((TAPS * 8, 128), jnp.float32),
                pltpu.VMEM((CLASSES * 8, 128), jnp.float32),
                pltpu.VMEM((TAPS * ROWS, 128), jnp.float32),
                pltpu.VMEM((ITERS, 2, 5, ROWS, 128), jnp.float32),
                pltpu.VMEM((ITERS, 2, ROWS, 128), jnp.float32),
                pltpu.VMEM((3 * TILE, 128), jnp.float32),
            ],
        ),
        out_shape=[
            jax.ShapeDtypeStruct(kernels.shape, jnp.bfloat16),
            jax.ShapeDtypeStruct((amount, 8, 128), jnp.float32),
        ],
        compiler_params=pltpu.CompilerParams(vmem_limit_bytes=24 * 1024 * 1024),
    )(listed, kernels, unary, target)


def on_device(fk, fu, fl, fm, dest, slot, rk, ru, rl, rm):
    destinations, slots = dest[0, 0], slot[0, 0]
    flag_grad, partial = crf(destinations, fk, fu, fl, fm)
    count = lax.axis_size("length")
    losses = jnp.sum(partial, axis=(1, 2)) / TILE
    place = jnp.where(destinations >= 0, destinations * RECV + slots, -1)
    table = jnp.sum(
        jnp.where(place[None, :] == jnp.arange(count * RECV)[:, None], losses[None, :], 0.0), axis=1
    )
    got = lax.all_to_all(
        table.reshape(count, RECV), "length", split_axis=0, concat_axis=0, tiled=True
    )
    res_grad, _ = crf(jnp.zeros((rk.shape[2],), jnp.int32), rk, ru, rl, rm)
    return flag_grad, res_grad, jnp.sum(got, axis=0)[None, None]


def solution(mesh):
    tile_axes = ("groups", "sector", "pair")
    spec = lambda n: P("length", tile_axes, *([None] * n))
    return jax.shard_map(
        on_device,
        mesh=mesh,
        in_specs=(spec(3), spec(3), spec(2), spec(2), spec(1), spec(1), spec(3), spec(3), spec(2), spec(2)),
        out_specs=(spec(3), spec(3), spec(1)),
        check_vma=False,
    )
```

```python
import functools

import jax
import jax.numpy as jnp
from jax import lax
from jax.experimental import pallas as pl
from jax.experimental.pallas import tpu as pltpu
from jax.sharding import PartitionSpec as P

CLASSES = 8
TAPS = 25
TILE = 32
ITERS = 3
RECV = 16
BATCH = 16

OFFSETS = [(a, b) for a in range(-2, 3) for b in range(-2, 3)]


def shift_all(x, lane):
    after = pltpu.roll(x, 7, 0)
    before = pltpu.roll(x, 1, 0)
    shifted = []
    for a, b in OFFSETS:
        k = a * TILE + b
        if k == 0:
            shifted.append(x)
        elif k > 0:
            shifted.append(pltpu.roll(jnp.where(lane >= k, x, after), 128 - k, 1))
        else:
            shifted.append(pltpu.roll(jnp.where(lane < 128 + k, x, before), -k, 1))
    return shifted


def shift_one(x, k, lane):
    if k == 0:
        return x
    if k > 0:
        return pltpu.roll(jnp.where(lane >= k, x, pltpu.roll(x, 7, 0)), 128 - k, 1)
    return pltpu.roll(jnp.where(lane < 128 + k, x, pltpu.roll(x, 1, 0)), -k, 1)


def total(values):
    while len(values) > 1:
        values = [sum(values[i : i + 2]) for i in range(0, len(values), 2)]
    return values[0]


def tile(j, tgt_ref, loss_ref, flat, unary, kfwd, kbwd, shf):
    lane = lax.broadcasted_iota(jnp.int32, (8, 128), 1)
    sub = lax.broadcasted_iota(jnp.int32, (8, 128), 0)
    row = sub * 4 + lane // TILE
    col = lane % TILE

    def inside(t):
        a, b = OFFSETS[t]
        return (row + a >= 0) & (row + a < TILE) & (col + b >= 0) & (col + b < TILE)

    for t in range(TAPS):
        a, b = OFFSETS[t]
        masked = jnp.where(inside(t), flat[pl.ds(pl.multiple_of(j * (TAPS * 8) + 8 * t, 8), 8), :], 0.0)
        kfwd[t] = masked
        kbwd[TAPS - 1 - t] = shift_one(masked, -(a * TILE + b), lane)

    def send(field, weights, keep):
        result = []
        for c in range(CLASSES):
            moved = shift_all(field[c], lane)
            if keep is not None:
                for t in range(TAPS):
                    shf[keep, t, c] = moved[t]
            sums = [moved[t] * weights[t] for t in range(5)]
            for t in range(5, TAPS):
                sums[t % 5] = sums[t % 5] + moved[t] * weights[t]
            result.append(total(sums))
        return result

    def soft(logits):
        raised = [jnp.exp(x) for x in logits]
        summed = total(raised)
        scale = 1.0 / summed
        return [x * scale for x in raised], summed

    first = [unary[pl.ds(pl.multiple_of(j * (CLASSES * 8) + 8 * c, 8), 8), :] for c in range(CLASSES)]
    beliefs, _ = soft(first)
    kept = [beliefs]
    for i in range(ITERS):
        sent = send(beliefs, kfwd, i)
        logits = [unary[pl.ds(pl.multiple_of(j * (CLASSES * 8) + 8 * c, 8), 8), :] + sent[c] for c in range(CLASSES)]
        beliefs, summed = soft(logits)
        kept.append(beliefs)
    labels = tgt_ref[j]
    used = labels < CLASSES
    chosen = total([jnp.where(labels == c, logits[c], 0.0) for c in range(CLASSES)])
    loss_ref[j] = jnp.where(used, jnp.log(summed) - chosen, 0.0)
    slope = [
        jnp.where(used, kept[3][c] - jnp.where(labels == c, 1.0, 0.0), 0.0)
        for c in range(CLASSES)
    ]
    slopes = [None, None, slope]
    for i in (1, 0):
        back = send(slopes[i + 1], kbwd, None)
        field = kept[i + 1]
        mean = total([field[c] * back[c] for c in range(CLASSES)])
        slopes[i] = [field[c] * (back[c] - mean) for c in range(CLASSES)]
    for t in range(TAPS):
        gathered = total(
            [slopes[i][c] * shf[i, t, c] for i in range(ITERS) for c in range(CLASSES)]
        )
        flat[pl.ds(pl.multiple_of(j * (TAPS * 8) + 8 * t, 8), 8), :] = jnp.where(inside(t), gathered, 0.0)


def crf_kernel(dest_ref, k_ref, u_ref, tgt_ref, grad_ref, loss_ref, *scratch):
    step = tgt_ref.shape[0]
    base = pl.program_id(0) * step
    flat, unary = scratch[:2]
    for p in range(8):
        part = slice(128 * p, 128 * (p + 1))
        for t in range(TAPS):
            flat[pl.ds(8 * t + p, step, stride=8 * TAPS), :] = k_ref[0, 0, t, :, part].astype(
                jnp.float32
            )

    @pl.loop(0, step)
    def _(j):
        listed = dest_ref[base + j] >= 0

        @pl.when(listed)
        def _():
            for p in range(8):
                part = slice(128 * p, 128 * (p + 1))
                start = j * (CLASSES * 8) + p
                unary[pl.ds(start, CLASSES, stride=8), :] = u_ref[0, 0, j, :, part].astype(
                    jnp.float32
                )
            tile(j, tgt_ref, loss_ref, *scratch)

        @pl.when(jnp.logical_not(listed))
        def _():
            start = pl.multiple_of(j * (TAPS * 8), 8)
            flat[pl.ds(start, TAPS * 8), :] = jnp.zeros((TAPS * 8, 128), jnp.float32)
            loss_ref[j] = jnp.zeros((8, 128), jnp.float32)

    for p in range(8):
        part = slice(128 * p, 128 * (p + 1))
        for t in range(TAPS):
            grad_ref[0, 0, t, :, part] = flat[
                pl.ds(8 * t + p, step, stride=8 * TAPS), :
            ].astype(jnp.bfloat16)


def crf(listed, kernels, unary, labels, mask):
    amount, taps, pixels = kernels.shape[2:]
    step = min(BATCH, amount)
    kernels = jnp.swapaxes(kernels, 2, 3)
    taps_first = pl.BlockSpec((1, 1, taps, step, pixels), lambda i, s: (0, 0, 0, i, 0))
    scores = pl.BlockSpec((1, 1, step, CLASSES, pixels), lambda i, s: (0, 0, i, 0, 0))
    fields = pl.BlockSpec((step, 8, 128), lambda i, s: (i, 0, 0))
    target = jnp.where(mask == 1, labels, CLASSES).reshape(amount, 8, 128)
    grad, loss = pl.pallas_call(
        crf_kernel,
        grid_spec=pltpu.PrefetchScalarGridSpec(
            num_scalar_prefetch=1,
            grid=(amount // step,),
            in_specs=[taps_first, scores, fields],
            out_specs=[taps_first, fields],
            scratch_shapes=[
                pltpu.VMEM((step * TAPS * 8, 128), jnp.float32),
                pltpu.VMEM((step * CLASSES * 8, 128), jnp.float32),
                pltpu.VMEM((TAPS, 8, 128), jnp.float32),
                pltpu.VMEM((TAPS, 8, 128), jnp.float32),
                pltpu.VMEM((ITERS, TAPS, CLASSES, 8, 128), jnp.float32),
            ],
        ),
        out_shape=[
            jax.ShapeDtypeStruct(kernels.shape, jnp.bfloat16),
            jax.ShapeDtypeStruct((amount, 8, 128), jnp.float32),
        ],
        compiler_params=pltpu.CompilerParams(vmem_limit_bytes=32 * 1024 * 1024),
    )(listed, kernels, unary, target)
    return jnp.swapaxes(grad, 2, 3), loss


def on_device(fk, fu, fl, fm, dest, slot, rk, ru, rl, rm):
    destinations, slots = dest[0, 0], slot[0, 0]
    flag_grad, partial = crf(destinations, fk, fu, fl, fm)
    count = lax.axis_size("length")
    losses = jnp.sum(partial, axis=(1, 2)) / TILE
    place = jnp.where(destinations >= 0, destinations * RECV + slots, -1)
    table = jnp.sum(
        jnp.where(place[None, :] == jnp.arange(count * RECV)[:, None], losses[None, :], 0.0), axis=1
    )
    got = lax.all_to_all(
        table.reshape(count, RECV), "length", split_axis=0, concat_axis=0, tiled=True
    )
    res_grad, _ = crf(jnp.zeros((rk.shape[2],), jnp.int32), rk, ru, rl, rm)
    return flag_grad, res_grad, jnp.sum(got, axis=0)[None, None]


def solution(mesh):
    tile_axes = ("groups", "sector", "pair")
    spec = lambda n: P("length", tile_axes, *([None] * n))
    return jax.shard_map(
        on_device,
        mesh=mesh,
        in_specs=(spec(3), spec(3), spec(2), spec(2), spec(1), spec(1), spec(3), spec(3), spec(2), spec(2)),
        out_specs=(spec(3), spec(3), spec(1)),
        check_vma=False,
    )
```

```python
import functools

import jax
import jax.numpy as jnp
from jax import lax
from jax.experimental import pallas as pl
from jax.experimental.pallas import tpu as pltpu
from jax.sharding import PartitionSpec as P

CLASSES = 8
TAPS = 25
TILE = 32
ITERS = 3
RECV = 16
BATCH = 16
TOGETHER = 2

OFFSETS = [(a, b) for a in range(-2, 3) for b in range(-2, 3)]


def shift_all(x, lane):
    after = pltpu.roll(x, 7, 0)
    before = pltpu.roll(x, 1, 0)
    shifted = []
    for a, b in OFFSETS:
        k = a * TILE + b
        if k == 0:
            shifted.append(x)
        elif k > 0:
            shifted.append(pltpu.roll(jnp.where(lane >= k, x, after), 128 - k, 1))
        else:
            shifted.append(pltpu.roll(jnp.where(lane < 128 + k, x, before), -k, 1))
    return shifted


def shift_one(x, k, lane):
    if k == 0:
        return x
    if k > 0:
        return pltpu.roll(jnp.where(lane >= k, x, pltpu.roll(x, 7, 0)), 128 - k, 1)
    return pltpu.roll(jnp.where(lane < 128 + k, x, pltpu.roll(x, 1, 0)), -k, 1)


def total(values):
    while len(values) > 1:
        values = [sum(values[i : i + 2]) for i in range(0, len(values), 2)]
    return values[0]


def tile(j, tgt_ref, loss_ref, flat, unary, kfwd, kbwd, shf):
    lane = lax.broadcasted_iota(jnp.int32, (8, 128), 1)
    sub = lax.broadcasted_iota(jnp.int32, (8, 128), 0)
    row = sub * 4 + lane // TILE
    col = lane % TILE

    def inside(t):
        a, b = OFFSETS[t]
        return (row + a >= 0) & (row + a < TILE) & (col + b >= 0) & (col + b < TILE)

    for t in range(TAPS):
        a, b = OFFSETS[t]
        masked = jnp.where(inside(t), flat[pl.ds(pl.multiple_of(j * (TAPS * 8) + 8 * t, 8), 8), :], 0.0)
        kfwd[t] = masked
        kbwd[TAPS - 1 - t] = shift_one(masked, -(a * TILE + b), lane)

    yield

    def send(field, weights, keep):
        result = []
        for c in range(CLASSES):
            moved = shift_all(field[c], lane)
            if keep is not None:
                for t in range(TAPS):
                    shf[keep, t, c] = moved[t]
            sums = [moved[t] * weights[t] for t in range(5)]
            for t in range(5, TAPS):
                sums[t % 5] = sums[t % 5] + moved[t] * weights[t]
            result.append(total(sums))
        return result

    def soft(logits):
        raised = [jnp.exp(x) for x in logits]
        summed = total(raised)
        scale = 1.0 / summed
        return [x * scale for x in raised], summed

    first = [unary[pl.ds(pl.multiple_of(j * (CLASSES * 8) + 8 * c, 8), 8), :] for c in range(CLASSES)]
    beliefs, _ = soft(first)
    kept = [beliefs]
    for i in range(ITERS):
        sent = send(beliefs, kfwd, i)
        yield
        logits = [unary[pl.ds(pl.multiple_of(j * (CLASSES * 8) + 8 * c, 8), 8), :] + sent[c] for c in range(CLASSES)]
        beliefs, summed = soft(logits)
        yield
        kept.append(beliefs)
    labels = tgt_ref[j]
    used = labels < CLASSES
    chosen = total([jnp.where(labels == c, logits[c], 0.0) for c in range(CLASSES)])
    loss_ref[j] = jnp.where(used, jnp.log(summed) - chosen, 0.0)
    slope = [
        jnp.where(used, kept[3][c] - jnp.where(labels == c, 1.0, 0.0), 0.0)
        for c in range(CLASSES)
    ]
    slopes = [None, None, slope]
    for i in (1, 0):
        back = send(slopes[i + 1], kbwd, None)
        yield
        field = kept[i + 1]
        mean = total([field[c] * back[c] for c in range(CLASSES)])
        slopes[i] = [field[c] * (back[c] - mean) for c in range(CLASSES)]
        yield
    for t in range(TAPS):
        chains = [slopes[0][c] * shf[0, t, c] for c in range(4)]
        for n in range(4, ITERS * CLASSES):
            i, c = n // CLASSES, n % CLASSES
            chains[n % 4] = chains[n % 4] + slopes[i][c] * shf[i, t, c]
        gathered = total(chains)
        flat[pl.ds(pl.multiple_of(j * (TAPS * 8) + 8 * t, 8), 8), :] = jnp.where(inside(t), gathered, 0.0)


def crf_kernel(dest_ref, k_ref, u_ref, tgt_ref, grad_ref, loss_ref, *scratch):
    step = tgt_ref.shape[0]
    base = pl.program_id(0) * step
    flat, unary = scratch[:2]
    for p in range(8):
        part = slice(128 * p, 128 * (p + 1))
        for t in range(TAPS):
            flat[pl.ds(8 * t + p, step, stride=8 * TAPS), :] = k_ref[0, 0, t, :, part].astype(
                jnp.float32
            )

    def clear(j):
        start = pl.multiple_of(j * (TAPS * 8), 8)
        flat[pl.ds(start, TAPS * 8), :] = jnp.zeros((TAPS * 8, 128), jnp.float32)
        loss_ref[j] = jnp.zeros((8, 128), jnp.float32)

    @pl.loop(0, step // TOGETHER)
    def _(n):
        members = [n * TOGETHER + w for w in range(TOGETHER)]
        listed = [dest_ref[base + j] >= 0 for j in members]

        @pl.when(functools.reduce(jnp.logical_or, listed))
        def _():
            for j in members:
                for p in range(8):
                    part = slice(128 * p, 128 * (p + 1))
                    start = j * (CLASSES * 8) + p
                    unary[pl.ds(start, CLASSES, stride=8), :] = u_ref[0, 0, j, :, part].astype(
                        jnp.float32
                    )
            steps = [
                tile(j, tgt_ref, loss_ref, flat, unary, *[ref.at[w] for ref in scratch[2:]])
                for w, j in enumerate(members)
            ]
            for _ in zip(*steps):
                pass
            for rest in steps[1:]:
                for _ in rest:
                    pass

        for j, known in zip(members, listed):
            pl.when(jnp.logical_not(known))(functools.partial(clear, j))

    for p in range(8):
        part = slice(128 * p, 128 * (p + 1))
        for t in range(TAPS):
            grad_ref[0, 0, t, :, part] = flat[
                pl.ds(8 * t + p, step, stride=8 * TAPS), :
            ].astype(jnp.bfloat16)


def crf(listed, kernels, unary, labels, mask):
    amount, taps, pixels = kernels.shape[2:]
    step = min(BATCH, amount)
    kernels = jnp.swapaxes(kernels, 2, 3)
    taps_first = pl.BlockSpec((1, 1, taps, step, pixels), lambda i, s: (0, 0, 0, i, 0))
    scores = pl.BlockSpec((1, 1, step, CLASSES, pixels), lambda i, s: (0, 0, i, 0, 0))
    fields = pl.BlockSpec((step, 8, 128), lambda i, s: (i, 0, 0))
    target = jnp.where(mask == 1, labels, CLASSES).reshape(amount, 8, 128)
    grad, loss = pl.pallas_call(
        crf_kernel,
        grid_spec=pltpu.PrefetchScalarGridSpec(
            num_scalar_prefetch=1,
            grid=(amount // step,),
            in_specs=[taps_first, scores, fields],
            out_specs=[taps_first, fields],
            scratch_shapes=[
                pltpu.VMEM((step * TAPS * 8, 128), jnp.float32),
                pltpu.VMEM((step * CLASSES * 8, 128), jnp.float32),
                pltpu.VMEM((TOGETHER, TAPS, 8, 128), jnp.float32),
                pltpu.VMEM((TOGETHER, TAPS, 8, 128), jnp.float32),
                pltpu.VMEM((TOGETHER, ITERS, TAPS, CLASSES, 8, 128), jnp.float32),
            ],
        ),
        out_shape=[
            jax.ShapeDtypeStruct(kernels.shape, jnp.bfloat16),
            jax.ShapeDtypeStruct((amount, 8, 128), jnp.float32),
        ],
        compiler_params=pltpu.CompilerParams(vmem_limit_bytes=32 * 1024 * 1024),
    )(listed, kernels, unary, target)
    return jnp.swapaxes(grad, 2, 3), loss


def on_device(fk, fu, fl, fm, dest, slot, rk, ru, rl, rm):
    destinations, slots = dest[0, 0], slot[0, 0]
    flag_grad, partial = crf(destinations, fk, fu, fl, fm)
    count = lax.axis_size("length")
    losses = jnp.sum(partial, axis=(1, 2)) / TILE
    place = jnp.where(destinations >= 0, destinations * RECV + slots, -1)
    table = jnp.sum(
        jnp.where(place[None, :] == jnp.arange(count * RECV)[:, None], losses[None, :], 0.0), axis=1
    )
    got = lax.all_to_all(
        table.reshape(count, RECV), "length", split_axis=0, concat_axis=0, tiled=True
    )
    res_grad, _ = crf(jnp.zeros((rk.shape[2],), jnp.int32), rk, ru, rl, rm)
    return flag_grad, res_grad, jnp.sum(got, axis=0)[None, None]


def solution(mesh):
    tile_axes = ("groups", "sector", "pair")
    spec = lambda n: P("length", tile_axes, *([None] * n))
    return jax.shard_map(
        on_device,
        mesh=mesh,
        in_specs=(spec(3), spec(3), spec(2), spec(2), spec(1), spec(1), spec(3), spec(3), spec(2), spec(2)),
        out_specs=(spec(3), spec(3), spec(1)),
        check_vma=False,
    )
```
